256 devices in a mesh: station: 64 (over y, x_lo, z), tblock: 4 (over x_hi, core).
Axes of the slice: x: 4 (x_hi: 2, x_lo: 2; x = x_hi * 2 + x_lo), y: 4, z: 8, core: 2. Of those that a mesh axis runs over, the one named last changes fastest.
Arguments:
- voltages: bfloat16 [2, 1024, 262144], P(None, 'station', 'tblock'), may hold values from -127 to 127, as said below
- prototype: float32 [4, 4096], replicated, may hold values from -1.5 to 1.5
Outputs:
- visibilities: bfloat16 [256, 2, 1024, 1024], P(('station', 'tblock'))
The draws below stay inside these ranges and needn't reach their ends.
Inputs may be any that keep to these rules, and one draw needn't show every extreme that they name: `voltages`: integer-valued samples.
All inputs are finite; a program needn't handle non-finite values.
Results may differ from the reference program's by a relative error of at most 0.0088.
Values may be sent and summed in bfloat16 or wider, within the bound.
A program may use at most 192 MiB of HBM per device.

```python
import math
import jax
import jax.numpy as jnp
from jax import lax

INPUTS = 1024
ROOT = 64
NFFT = 4096
TAPS = 4
SPECTRA = 64
BAND = 256
SAMPLES = 262144


def draw_voltages(key, part):
    key = jax.random.fold_in(key, 7)
    levels = jax.random.randint(key, (2, INPUTS, SAMPLES), -127, 128)
    levels = levels.at[0, 0, 0].set(-127).at[1, 0, 0].set(127)
    return levels.astype(jnp.float32).astype(jnp.bfloat16)


def normal_values(own_key, shape, scale, bound, kind=jnp.bfloat16):
    values = jax.random.normal(own_key, shape, jnp.float32) * scale
    return jnp.minimum(jnp.maximum(values, -bound), bound).astype(kind)


def setup_inputs(seed: int = 0) -> dict:
    key_list = jax.random.split(jax.random.key(seed), 3)
    return {
        "voltages": draw_voltages(jax.random.fold_in(key_list[2], 71), 0),
        "prototype": normal_values(key_list[1], (TAPS, NFFT), 0.25, 1.5, jnp.float32),
    }


def angles(first_index, second_index, period):
    product = (first_index[:, None] * second_index[None, :]) % period
    return product.astype(jnp.float32) * (2.0 * math.pi / period)


def transform(subscripts, left_side, table):
    return jnp.einsum(subscripts, left_side.astype(jnp.float32), table.astype(jnp.float32), precision=lax.Precision.HIGHEST)


def channel_band(filtered, band_width):
    inputs_here = filtered.shape[1]
    frames = filtered.shape[2]
    points = filtered.shape[3]
    root_size = ROOT
    folded = filtered.reshape(2, inputs_here, frames, root_size, root_size)
    digits = jnp.arange(root_size, dtype=jnp.int32)
    first_angle = angles(digits, digits, root_size)
    cos_first = jnp.cos(first_angle).astype(jnp.bfloat16)
    sin_first = jnp.sin(first_angle).astype(jnp.bfloat16)
    real_section = transform("psab,ac->psbc", folded[0], cos_first) + transform("psab,ac->psbc", folded[1], sin_first)
    imag_section = transform("psab,ac->psbc", folded[1], cos_first) - transform("psab,ac->psbc", folded[0], sin_first)
    twist_angle = angles(digits, digits, points)
    cos_twist = jnp.cos(twist_angle)
    sin_twist = jnp.sin(twist_angle)
    real_turned = (real_section * cos_twist + imag_section * sin_twist).astype(jnp.bfloat16)
    imag_turned = (imag_section * cos_twist - real_section * sin_twist).astype(jnp.bfloat16)
    lower_edge = (points - band_width) // 2
    first_digit = lower_edge // root_size
    last_digit = (lower_edge + band_width - 1) // root_size
    digit_count = last_digit - first_digit + 1
    high_digits = first_digit + jnp.arange(digit_count, dtype=jnp.int32)
    second_angle = angles(digits, high_digits, root_size)
    cos_second = jnp.cos(second_angle).astype(jnp.bfloat16)
    sin_second = jnp.sin(second_angle).astype(jnp.bfloat16)
    real_out = transform("psbc,bd->sdcp", real_turned, cos_second) + transform("psbc,bd->sdcp", imag_turned, sin_second)
    imag_out = transform("psbc,bd->sdcp", imag_turned, cos_second) - transform("psbc,bd->sdcp", real_turned, sin_second)
    spectra_all = jnp.stack([real_out, imag_out]).reshape(2, frames, digit_count * root_size, inputs_here)
    offset_start = lower_edge - first_digit * root_size
    return spectra_all[:, :, offset_start:offset_start + band_width, :]


def reference(voltages, prototype):
    scale = 1.0 / (32.0 * ROOT)

    def channelize(samples):
        wide = samples.astype(jnp.float32)
        padded = jnp.concatenate([jnp.zeros((2, (TAPS - 1) * NFFT), jnp.float32), wide], axis=1)
        framed = padded.reshape(2, SPECTRA + TAPS - 1, NFFT)
        filtered = jnp.zeros((2, SPECTRA, NFFT), jnp.float32)
        for tap_index in range(TAPS):
            filtered = filtered + prototype[tap_index] * framed[:, tap_index:tap_index + SPECTRA, :]
        rounded = filtered.astype(jnp.bfloat16).reshape(2, 1, SPECTRA, NFFT)
        band_values = channel_band(rounded, BAND)[:, :, :, 0]
        return (band_values * scale).astype(jnp.bfloat16)

    per_input = lax.map(channelize, jnp.moveaxis(voltages, 1, 0))
    per_channel = jnp.transpose(per_input, (3, 1, 0, 2))

    def correlate(channel_block):
        stacked = jnp.concatenate([channel_block[0], channel_block[1]], axis=1)
        turned = jnp.concatenate([channel_block[1], -channel_block[0]], axis=1)
        real_vis = jnp.dot(stacked, stacked.T, preferred_element_type=jnp.float32)
        imag_vis = jnp.dot(turned, stacked.T, preferred_element_type=jnp.float32)
        return (jnp.stack([real_vis, imag_vis]) / SPECTRA).astype(jnp.bfloat16)

    return lax.map(correlate, per_channel)
```

```python
import math

import jax
import jax.numpy as jnp
import ml_dtypes
import numpy as np
from jax import lax
from jax.experimental import pallas as pl
from jax.experimental.pallas import tpu as pltpu
from jax.sharding import PartitionSpec as P

ROOT = 64
NFFT = 4096
TAPS = 4
BAND = 256
FRAMES = 16
INPUTS = 16
ROWS = FRAMES * INPUTS
EDGE = TAPS - 1
EDGE_ROWS = 64
STATIONS = 64
BLOCKS = 4
DEVICES = STATIONS * BLOCKS
LANES = 128
STEP = 128
MESH = pl.DeviceIdType.MESH


def channel_table():
    def angles(first, second, period):
        product = (first[:, None] * second[None, :]) % period
        return product.astype(np.float32) * np.float32(2.0 * math.pi / period)

    def rounded(values):
        return values.astype(ml_dtypes.bfloat16).astype(np.float64)

    digits = np.arange(ROOT)
    first = angles(digits, digits, ROOT)
    root = rounded(np.cos(first)) - 1j * rounded(np.sin(first))
    twist_angle = angles(digits, digits, NFFT)
    twist = np.cos(twist_angle).astype(np.float64) - 1j * np.sin(twist_angle).astype(np.float64)
    high = (NFFT - BAND) // 2 // ROOT + np.arange(BAND // ROOT)
    table = (
        root.T[None, :, :, None] * twist.T[None, :, None, :] * root[:, high].T[:, None, None, :]
    )
    table = table.reshape(BAND, NFFT) / (32.0 * ROOT)
    return np.concatenate([table.real, table.imag]).astype(np.float32).astype(ml_dtypes.bfloat16)


def device(index):
    return (lax.div(index, BLOCKS), lax.rem(index, BLOCKS))


def exchange_kernel(
    v_hbm,
    proto_ref,
    w_hbm,
    out_ref,
    v_buf,
    w_buf,
    x_buf,
    xe_buf,
    rows_buf,
    edge_out,
    edge_in,
    send_buf,
    v_sem,
    w_sem,
    edge_send,
    edge_recv,
    send_sem,
    recv_sem,
):
    station = lax.axis_index("station")
    block = lax.axis_index("tblock")
    me = station * BLOCKS + block

    frame_order = list(range(FRAMES - EDGE, FRAMES)) + list(range(FRAMES - EDGE))
    frame_copies = {}
    for f in frame_order:
        here = pl.ds(f * NFFT, NFFT)
        frame_copies[f] = pltpu.make_async_copy(
            v_hbm.at[:, :, here], v_buf.at[:, :, here], v_sem.at[f]
        )
        frame_copies[f].start()
    w_copy = pltpu.make_async_copy(w_hbm, w_buf, w_sem)
    w_copy.start()

    barrier = pltpu.get_barrier_semaphore()

    def greet(k, carry):
        other = lax.rem(me + k, DEVICES)
        pl.semaphore_signal(barrier, inc=1, device_id=device(other), device_id_type=MESH)
        return carry

    lax.fori_loop(1, DEVICES, greet, 0, unroll=5)

    for f in frame_order:
        frame_copies[f].wait()

    def filter_step(k, carry):
        lanes = pl.ds(pl.multiple_of(k * STEP, STEP), STEP)
        taps = [proto_ref[pl.ds(t, 1), lanes] for t in range(TAPS)]
        for part in range(2):
            window = {}
            for s in range(FRAMES + EDGE):
                if s < FRAMES:
                    at = pl.ds(pl.multiple_of(s * NFFT + k * STEP, STEP), STEP)
                    window[s] = v_buf[part, :, at].astype(jnp.float32)
                total = None
                for t in range(TAPS):
                    f = s + t - EDGE
                    if 0 <= f < FRAMES:
                        term = taps[t] * window[f]
                        total = term if total is None else total + term
                value = total.astype(jnp.bfloat16)
                if s < FRAMES:
                    x_buf[pl.ds(part * ROWS + s * INPUTS, INPUTS), lanes] = value
                else:
                    row = part * EDGE_ROWS + (s - FRAMES) * INPUTS
                    xe_buf[pl.ds(row, INPUTS), lanes] = value
            pad = part * EDGE_ROWS + EDGE * INPUTS
            xe_buf[pl.ds(pad, INPUTS), lanes] = jnp.zeros((INPUTS, STEP), jnp.bfloat16)
        return carry

    lax.fori_loop(0, NFFT // STEP, filter_step, 0)

    w_copy.wait()
    contract = (((1,), (1,)), ((), ()))
    edge = lax.dot_general(w_buf[...], xe_buf[...], contract, preferred_element_type=jnp.float32)
    lane = lax.broadcasted_iota(jnp.int32, (BAND, LANES), 1)
    turned = pltpu.roll(edge[BAND:], EDGE_ROWS, 1)
    edge = edge[:BAND] + jnp.where(lane < EDGE_ROWS, -turned, turned)
    edge_out[...] = edge.astype(jnp.bfloat16)

    pl.semaphore_wait(barrier, DEVICES - 1)

    after = (station, lax.min(block + 1, BLOCKS - 1))
    edge_copy = pltpu.make_async_remote_copy(
        src_ref=edge_out,
        dst_ref=edge_in,
        send_sem=edge_send,
        recv_sem=edge_recv,
        device_id=after,
        device_id_type=MESH,
    )

    @pl.when(block < BLOCKS - 1)
    def _():
        edge_copy.start()

    @pl.when(block == 0)
    def _():
        edge_in[...] = jnp.zeros_like(edge_in)

    main = lax.dot_general(w_buf[...], x_buf[...], contract, preferred_element_type=jnp.float32)
    real = main[:BAND, :ROWS] - main[BAND:, ROWS:]
    imag = main[BAND:, :ROWS] + main[:BAND, ROWS:]

    @pl.when(block > 0)
    def _():
        edge_copy.wait_recv()

    carried = edge_in[...].astype(jnp.float32)
    real_edge = jnp.where(lane < EDGE_ROWS, carried, 0.0)
    imag_edge = jnp.where(lane < EDGE_ROWS, pltpu.roll(carried, EDGE_ROWS, 1), 0.0)
    pieces = [
        real[:, :LANES] + real_edge,
        real[:, LANES:],
        imag[:, :LANES] + imag_edge,
        imag[:, LANES:],
    ]
    for r in range(4):
        rows_buf[pl.ds(r, BAND, stride=4), :] = pieces[r]
    send_buf[...] = rows_buf[...].reshape(BAND, 4, LANES).astype(jnp.bfloat16)

    own = pltpu.make_async_copy(send_buf.at[me], out_ref.at[me], recv_sem)
    own.start()

    def go(k, carry):
        other = lax.rem(me + k, DEVICES)
        pltpu.make_async_remote_copy(
            src_ref=send_buf.at[other],
            dst_ref=out_ref.at[me],
            send_sem=send_sem,
            recv_sem=recv_sem,
            device_id=device(other),
            device_id_type=MESH,
        ).start()
        return carry

    lax.fori_loop(1, DEVICES, go, 0, unroll=5)

    @pl.when(block < BLOCKS - 1)
    def _():
        edge_copy.wait_send()

    sent = send_buf.at[pl.ds(0, DEVICES - 1)]
    pltpu.make_async_copy(sent, sent, send_sem).wait()
    pltpu.make_async_copy(out_ref, out_ref, recv_sem).wait()


def exchange(voltages, prototype, table):
    return pl.pallas_call(
        exchange_kernel,
        out_shape=jax.ShapeDtypeStruct((DEVICES, 4, LANES), jnp.bfloat16),
        in_specs=[
            pl.BlockSpec(memory_space=pl.ANY),
            pl.BlockSpec(memory_space=pltpu.VMEM),
            pl.BlockSpec(memory_space=pl.ANY),
        ],
        out_specs=pl.BlockSpec(memory_space=pl.ANY),
        scratch_shapes=[
            pltpu.VMEM((2, INPUTS, FRAMES * NFFT), jnp.bfloat16),
            pltpu.VMEM((2 * BAND, NFFT), jnp.bfloat16),
            pltpu.VMEM((2 * ROWS, NFFT), jnp.bfloat16),
            pltpu.VMEM((2 * EDGE_ROWS, NFFT), jnp.bfloat16),
            pltpu.VMEM((4 * BAND, LANES), jnp.float32),
            pltpu.VMEM((BAND, LANES), jnp.bfloat16),
            pltpu.VMEM((BAND, LANES), jnp.bfloat16),
            pltpu.VMEM((DEVICES, 4, LANES), jnp.bfloat16),
            pltpu.SemaphoreType.DMA((FRAMES,)),
            pltpu.SemaphoreType.DMA,
            pltpu.SemaphoreType.DMA,
            pltpu.SemaphoreType.DMA,
            pltpu.SemaphoreType.DMA,
            pltpu.SemaphoreType.DMA,
        ],
        compiler_params=pltpu.CompilerParams(
            collective_id=0, has_side_effects=True, vmem_limit_bytes=40 * 1024 * 1024
        ),
        name="channelize_and_send",
    )(voltages, prototype, table)


def correlate_kernel(moved_ref, out_ref, wide, gathered, left, right):
    rows = out_ref.shape[2]
    step = pl.program_id(0)

    @pl.when(step == 0)
    def _():
        wide[...] = moved_ref[...].astype(jnp.float32).reshape(DEVICES * 4, LANES)
        spot = lax.broadcasted_iota(jnp.int32, (8, LANES), 1) // INPUTS
        row = lax.broadcasted_iota(jnp.int32, (8, LANES), 0)
        source = lax.rem(spot - row + 8, 8)
        back = lax.rem(lax.broadcasted_iota(jnp.int32, (8, LANES), 1) + row * INPUTS, LANES)
        for group in range(8):
            for q in range(16):
                tile = wide[pl.ds(group * 128 + q, 8, stride=16), :]
                tile = pltpu.roll(tile, 0, 1, stride=INPUTS, stride_axis=0)
                tile = jnp.take_along_axis(tile, source, axis=0)
                tile = jnp.take_along_axis(tile, back, axis=1)
                tb, part, half = q // 4, q // 2 % 2, q % 2
                at = part * 64 + (tb * 2 + half) * 8
                gathered[pl.ds(at, 8), pl.ds(group * LANES, LANES)] = tile
        right[...] = gathered[...].astype(jnp.bfloat16)
        lane = lax.broadcasted_iota(jnp.int32, (LANES, LANES), 1)
        for group in range(8):
            square = gathered[:, pl.ds(group * LANES, LANES)].T
            other = pltpu.roll(square, 64, 1)
            left[0, pl.ds(group * LANES, LANES), :] = square.astype(jnp.bfloat16)
            left[1, pl.ds(group * LANES, LANES), :] = jnp.where(lane < 64, other, -other).astype(
                jnp.bfloat16
            )

    here = pl.ds(pl.multiple_of(step * rows, rows), rows)
    for part in range(2):
        product = jnp.dot(left[part, here, :], right[...], preferred_element_type=jnp.float32)
        out_ref[0, part] = (product * (1.0 / 64.0)).astype(jnp.bfloat16)


def correlate(moved):
    everyone = STATIONS * INPUTS
    rows = 128
    return pl.pallas_call(
        correlate_kernel,
        grid=(everyone // rows,),
        out_shape=jax.ShapeDtypeStruct((1, 2, everyone, everyone), jnp.bfloat16),
        in_specs=[pl.BlockSpec((DEVICES, 4, LANES), lambda i: (0, 0, 0))],
        out_specs=pl.BlockSpec((1, 2, rows, everyone), lambda i: (0, 0, i, 0)),
        scratch_shapes=[
            pltpu.VMEM((DEVICES * 4, LANES), jnp.float32),
            pltpu.VMEM((LANES, everyone), jnp.float32),
            pltpu.VMEM((2, everyone, LANES), jnp.bfloat16),
            pltpu.VMEM((LANES, everyone), jnp.bfloat16),
        ],
        compiler_params=pltpu.CompilerParams(vmem_limit_bytes=32 * 1024 * 1024),
        name="correlate",
    )(moved)


def local(voltages, prototype):
    table = jnp.asarray(channel_table())
    return correlate(exchange(voltages, prototype, table))


def solution(mesh):
    return jax.shard_map(
        local,
        mesh=mesh,
        in_specs=(P(None, "station", "tblock"), P()),
        out_specs=P(("station", "tblock"), None, None, None),
        check_vma=False,
    )
```

```python
import math

import jax
import jax.numpy as jnp
import ml_dtypes
import numpy as np
from jax import lax
from jax.experimental import pallas as pl
from jax.experimental.pallas import tpu as pltpu
from jax.sharding import PartitionSpec as P

ROOT = 64
NFFT = 4096
TAPS = 4
BAND = 256
FRAMES = 16
INPUTS = 16
EDGE = TAPS - 1
QUAD = 4
QUAD_ROWS = QUAD * INPUTS
STATIONS = 64
BLOCKS = 4
DEVICES = STATIONS * BLOCKS
LANES = 128
CHUNK = 512
CHUNKS = NFFT // CHUNK
HALF = BAND // 2
MESH = pl.DeviceIdType.MESH
CONTRACT = (((1,), (1,)), ((), ()))


def channel_table():
    def angles(first, second, period):
        product = (first[:, None] * second[None, :]) % period
        return product.astype(np.float32) * np.float32(2.0 * math.pi / period)

    def rounded(values):
        return values.astype(ml_dtypes.bfloat16).astype(np.float64)

    digits = np.arange(ROOT)
    first = angles(digits, digits, ROOT)
    root = rounded(np.cos(first)) - 1j * rounded(np.sin(first))
    twist_angle = angles(digits, digits, NFFT)
    twist = np.cos(twist_angle).astype(np.float64) - 1j * np.sin(twist_angle).astype(np.float64)
    high = (NFFT - BAND) // 2 // ROOT + np.arange(BAND // ROOT)
    table = (
        root.T[None, :, :, None] * twist.T[None, :, None, :] * root[:, high].T[:, None, None, :]
    )
    table = table.reshape(BAND, NFFT) / (32.0 * ROOT)
    return np.concatenate([table.real, table.imag]).astype(np.float32).astype(ml_dtypes.bfloat16)


def far_first(step, size):
    return size // 2 + (1 - 2 * (step % 2)) * ((step + 1) // 2)


class Partners:
    def __init__(self):
        station = lax.axis_index("station")
        block = lax.axis_index("tblock")
        self.z = lax.rem(station, 8)
        x = lax.div(block, 2) * 2 + lax.rem(lax.div(station, 8), 2)
        y = lax.div(station, 16)
        core = lax.rem(block, 2)
        xs, ys = {}, {}
        for d in range(4):
            there = lax.rem(x + d, 4)
            xs[d] = (lax.rem(there, 2) * 8, lax.div(there, 2) * 2)
            ys[d] = lax.rem(y + d, 4) * 16
        offsets = [(dx, dy, dc) for dx in range(4) for dy in range(4) for dc in (1, 0)]
        offsets.sort(key=lambda o: -(min(o[0], 4 - o[0]) + min(o[1], 4 - o[1])))
        self.plane = []
        for dx, dy, dc in offsets:
            low, high = xs[dx]
            self.plane.append((ys[dy] + low, high + (core if dc == 0 else 1 - core)))

    def layer(self, step):
        if isinstance(step, int):
            shift = far_first(step, 8)
        else:
            odd = lax.rem(step, 2)
            shift = 4 + (1 - 2 * odd) * lax.div(step + 1, 2)
        z = lax.rem(self.z + shift, 8)
        found = [(base + z, block) for base, block in self.plane]
        return found[:-1] if isinstance(step, int) and step == 7 else found


def exchange_kernel(
    v_hbm,
    proto_hbm,
    w_hbm,
    late_out,
    early_out,
    proto_ref,
    v_buf,
    w_buf,
    x_even,
    x_odd,
    total,
    rows_buf,
    late_send,
    early_send,
    proto_sem,
    chunk_sem,
    late_send_sem,
    late_recv_sem,
    early_send_sem,
    early_recv_sem,
):
    station = lax.axis_index("station")
    block = lax.axis_index("tblock")
    me = station * BLOCKS + block
    slots = (x_even, x_odd)

    proto_copy = pltpu.make_async_copy(proto_hbm, proto_ref, proto_sem)
    proto_copy.start()
    for k in range(CHUNKS):
        lanes = pl.ds(k * CHUNK, CHUNK)
        pltpu.make_async_copy(w_hbm.at[:, lanes], w_buf.at[:, lanes], chunk_sem.at[k]).start()
        for f in range(FRAMES):
            here = pl.ds(f * NFFT + k * CHUNK, CHUNK)
            pltpu.make_async_copy(
                v_hbm.at[:, :, here], v_buf.at[:, :, here], chunk_sem.at[k]
            ).start()

    def chunk_wait(k):
        table_part = w_buf.at[:, pl.ds(0, CHUNK)]
        pltpu.make_async_copy(table_part, table_part, chunk_sem.at[k]).wait()
        frames_part = v_buf.at[:, :, pl.ds(0, FRAMES * CHUNK)]
        pltpu.make_async_copy(frames_part, frames_part, chunk_sem.at[k]).wait()

    barrier = pltpu.get_barrier_semaphore()

    def greet(k, carry):
        other = lax.rem(me + k, DEVICES)
        where = (lax.div(other, BLOCKS), lax.rem(other, BLOCKS))
        pl.semaphore_signal(barrier, inc=1, device_id=where, device_id_type=MESH)
        return carry

    lax.fori_loop(1, DEVICES, greet, 0, unroll=5)
    proto_copy.wait()

    def filter_chunk(k, slot, first, last):
        for tile in range(CHUNK // LANES):
            offset = k * CHUNK + tile * LANES
            offset = offset if isinstance(offset, int) else pl.multiple_of(offset, LANES)
            taps = [proto_ref[pl.ds(t, 1), pl.ds(offset, LANES)] for t in range(TAPS)]
            lanes = pl.ds(tile * LANES, LANES)
            for part in range(2):
                window = {}
                for s in range(first, last):
                    value = None
                    for t in range(TAPS):
                        f = s + t - EDGE
                        if 0 <= f < FRAMES:
                            if f not in window:
                                at = f * NFFT + offset
                                at = at if isinstance(at, int) else pl.multiple_of(at, LANES)
                                window[f] = v_buf[part, :, pl.ds(at, LANES)].astype(jnp.float32)
                            term = taps[t] * window[f]
                            value = term if value is None else value + term
                    group, place = (s - first) // QUAD, (s - first) % QUAD
                    row = (group * 2 + part) * QUAD_ROWS + place * INPUTS
                    if value is None:
                        value = jnp.zeros((INPUTS, LANES), jnp.float32)
                    slot[pl.ds(row, INPUTS), lanes] = value.astype(jnp.bfloat16)

    def product(k, slot, rows):
        offset = k * CHUNK
        offset = offset if isinstance(offset, int) else pl.multiple_of(offset, CHUNK)
        return lax.dot_general(
            w_buf[:, pl.ds(offset, CHUNK)],
            slot[pl.ds(0, rows), :],
            CONTRACT,
            preferred_element_type=jnp.float32,
        )

    lane = lax.broadcasted_iota(jnp.int32, (BAND, LANES), 1)

    def combined(column):
        lanes = pl.ds(column * LANES, LANES)
        turned = pltpu.roll(total[pl.ds(BAND, BAND), lanes], QUAD_ROWS, 1)
        return total[pl.ds(0, BAND), lanes] + jnp.where(lane < QUAD_ROWS, -turned, turned)

    late_rows = 4 * 2 * QUAD_ROWS
    chunk_wait(0)
    filter_chunk(0, slots[0], QUAD, FRAMES + QUAD)
    for k in range(CHUNKS):
        if k + 1 < CHUNKS:
            chunk_wait(k + 1)
            filter_chunk(k + 1, slots[(k + 1) % 2], QUAD, FRAMES + QUAD)
        added = product(k, slots[k % 2], late_rows)
        if k == 0:
            total[...] = added
        else:
            total[...] += added

    for column in range(4):
        rows_buf[pl.ds(column, BAND, stride=4), :] = combined(column)
    late_send[...] = rows_buf[...].reshape(BAND, 4, LANES).astype(jnp.bfloat16)

    pl.semaphore_wait(barrier, DEVICES - 1)
    partners = Partners()

    def send(found, source, target, send_sem, recv_sem):
        for where in found:
            pltpu.make_async_remote_copy(
                src_ref=source.at[where[0] * BLOCKS + where[1]],
                dst_ref=target.at[me],
                send_sem=send_sem,
                recv_sem=recv_sem,
                device_id=where,
                device_id_type=MESH,
            ).start()

    def send_late(step):
        send(partners.layer(step), late_send, late_out, late_send_sem, late_recv_sem)

    def send_early(step):
        send(partners.layer(step), early_send, early_out, early_send_sem, early_recv_sem)

    early_rows = 2 * QUAD_ROWS
    for k in range(CHUNKS):
        send_late(k)
        filter_chunk(k, slots[k % 2], 0, QUAD)
        added = product(k, slots[k % 2], early_rows)
        if k == 0:
            total[:, pl.ds(0, LANES)] = added
        else:
            total[:, pl.ds(0, LANES)] += added
    early_send[...] = combined(0).reshape(BAND, 1, LANES)

    def early_layer(step, carry):
        send_early(step)
        return carry

    lax.fori_loop(0, 7, early_layer, 0)
    send_early(7)
    own = [
        pltpu.make_async_copy(late_send.at[me], late_out.at[me], late_recv_sem),
        pltpu.make_async_copy(early_send.at[me], early_out.at[me], early_recv_sem),
    ]
    for copy in own:
        copy.start()

    for buffer, sem in ((late_send, late_send_sem), (early_send, early_send_sem)):
        sent = buffer.at[pl.ds(0, DEVICES - 1)]
        pltpu.make_async_copy(sent, sent, sem).wait()
    pltpu.make_async_copy(late_out, late_out, late_recv_sem).wait()
    pltpu.make_async_copy(early_out, early_out, early_recv_sem).wait()


def exchange(voltages, prototype, table):
    return pl.pallas_call(
        exchange_kernel,
        out_shape=(
            jax.ShapeDtypeStruct((DEVICES, 4, LANES), jnp.bfloat16),
            jax.ShapeDtypeStruct((DEVICES, 1, LANES), jnp.float32),
        ),
        in_specs=[pl.BlockSpec(memory_space=pltpu.HBM)] * 3,
        out_specs=(pl.BlockSpec(memory_space=pl.ANY),) * 2,
        scratch_shapes=[
            pltpu.VMEM((TAPS, NFFT), jnp.float32),
            pltpu.VMEM((2, INPUTS, FRAMES * NFFT), jnp.bfloat16),
            pltpu.VMEM((2 * BAND, NFFT), jnp.bfloat16),
            pltpu.VMEM((8 * QUAD_ROWS, CHUNK), jnp.bfloat16),
            pltpu.VMEM((8 * QUAD_ROWS, CHUNK), jnp.bfloat16),
            pltpu.VMEM((2 * BAND, 4 * LANES), jnp.float32),
            pltpu.VMEM((4 * BAND, LANES), jnp.float32),
            pltpu.VMEM((DEVICES, 4, LANES), jnp.bfloat16),
            pltpu.VMEM((DEVICES, 1, LANES), jnp.float32),
            pltpu.SemaphoreType.DMA,
            pltpu.SemaphoreType.DMA((CHUNKS,)),
            pltpu.SemaphoreType.DMA,
            pltpu.SemaphoreType.DMA,
            pltpu.SemaphoreType.DMA,
            pltpu.SemaphoreType.DMA,
        ],
        compiler_params=pltpu.CompilerParams(
            collective_id=0, has_side_effects=True, vmem_limit_bytes=32 * 1024 * 1024
        ),
        name="channelize_and_send",
    )(voltages, prototype, table)


def correlate_kernel(late_ref, early_ref, out_hbm, late, early, gathered, right, out_buf, out_sem):
    late[...] = late_ref[...].astype(jnp.float32).reshape(DEVICES * 4, LANES)
    early[...] = early_ref[...].reshape(DEVICES, LANES)
    lane = lax.broadcasted_iota(jnp.int32, (8, LANES), 1)
    row = lax.broadcasted_iota(jnp.int32, (8, LANES), 0)
    source = lax.rem(lane // INPUTS - row + 8, 8)
    back = lax.rem(lane + row * INPUTS, LANES)
    for group in range(8):
        columns = pl.ds(group * LANES, LANES)
        for block in range(BLOCKS):
            for quad in range(4):
                if quad > 0:
                    tile = late[pl.ds(group * 128 + block * 4 + quad - 1, 8, stride=16), :]
                else:
                    tile = early[pl.ds(group * 32 + block, 8, stride=4), :]
                    if block > 0:
                        tile = tile + late[pl.ds(group * 128 + block * 4 - 1, 8, stride=16), :]
                tile = pltpu.roll(tile, 0, 1, stride=INPUTS, stride_axis=0)
                tile = jnp.take_along_axis(tile, source, axis=0)
                tile = jnp.take_along_axis(tile, back, axis=1)
                at = (block * 4 + quad) * QUAD
                gathered[pl.ds(at, QUAD), columns] = tile[:QUAD]
                gathered[pl.ds(64 + at, QUAD), columns] = tile[QUAD:]
    right[...] = gathered[...].astype(jnp.bfloat16)

    wide = lax.broadcasted_iota(jnp.int32, (LANES, LANES), 1)
    copies = []
    for group in range(8):
        columns = pl.ds(group * LANES, LANES)
        square = gathered[:, columns].T
        other = pltpu.roll(square, 64, 1)
        other = jnp.where(wide < 64, other, -other)
        for part, left in enumerate((square, other)):
            product = jnp.dot(
                left.astype(jnp.bfloat16), right[...], preferred_element_type=jnp.float32
            )
            out_buf[0, part, columns, :] = (product * (1.0 / 64.0)).astype(jnp.bfloat16)
        copies.append(
            pltpu.make_async_copy(
                out_buf.at[:, :, columns, :], out_hbm.at[:, :, columns, :], out_sem.at[group]
            )
        )
        copies[-1].start()
    for copy in copies:
        copy.wait()


def correlate(late, early):
    everyone = STATIONS * INPUTS
    shape = (1, 2, everyone, everyone)
    return pl.pallas_call(
        correlate_kernel,
        out_shape=jax.ShapeDtypeStruct(shape, jnp.bfloat16),
        in_specs=[pl.BlockSpec(memory_space=pltpu.VMEM)] * 2,
        out_specs=pl.BlockSpec(memory_space=pltpu.HBM),
        scratch_shapes=[
            pltpu.VMEM((DEVICES * 4, LANES), jnp.float32),
            pltpu.VMEM((DEVICES, LANES), jnp.float32),
            pltpu.VMEM((LANES, everyone), jnp.float32),
            pltpu.VMEM((LANES, everyone), jnp.bfloat16),
            pltpu.VMEM(shape, jnp.bfloat16),
            pltpu.SemaphoreType.DMA((8,)),
        ],
        compiler_params=pltpu.CompilerParams(vmem_limit_bytes=32 * 1024 * 1024),
        name="correlate",
    )(late, early)


def local(voltages, prototype):
    table = jnp.asarray(channel_table())
    held = [pltpu.with_memory_space_constraint(x, pltpu.HBM) for x in (voltages, prototype, table)]
    return correlate(*exchange(*held))


def solution(mesh):
    return jax.shard_map(
        local,
        mesh=mesh,
        in_specs=(P(None, "station", "tblock"), P()),
        out_specs=P(("station", "tblock"), None, None, None),
        check_vma=False,
    )
```

```python
import math

import jax
import jax.numpy as jnp
import ml_dtypes
import numpy as np
from jax import lax
from jax.experimental import pallas as pl
from jax.experimental.pallas import tpu as pltpu
from jax.sharding import PartitionSpec as P

ROOT = 64
NFFT = 4096
TAPS = 4
BAND = 256
FRAMES = 16
INPUTS = 16
EDGE = TAPS - 1
QUAD = 4
QUAD_ROWS = QUAD * INPUTS
STATIONS = 64
BLOCKS = 4
DEVICES = STATIONS * BLOCKS
LANES = 128
HALF = NFFT // 2
PAIRS = BAND // 2
CHUNK = 512
CHUNKS = HALF // CHUNK
GROUPS = FRAMES // QUAD + 1
TILES = CHUNK // LANES
MESH = pl.DeviceIdType.MESH
CONTRACT = (((1,), (1,)), ((), ()))


def channel_table():
    def angles(first, second, period):
        product = (first[:, None] * second[None, :]) % period
        return product.astype(np.float32) * np.float32(2.0 * math.pi / period)

    def rounded(values):
        return values.astype(ml_dtypes.bfloat16).astype(np.float64)

    digits = np.arange(ROOT)
    first = angles(digits, digits, ROOT)
    root = rounded(np.cos(first)) - 1j * rounded(np.sin(first))
    twist_angle = angles(digits, digits, NFFT)
    twist = np.cos(twist_angle).astype(np.float64) - 1j * np.sin(twist_angle).astype(np.float64)
    high = (NFFT - BAND) // 2 // ROOT + np.arange(BAND // ROOT)
    table = (
        root.T[None, :, :, None] * twist.T[None, :, None, :] * root[:, high].T[:, None, None, :]
    )
    table = table.reshape(BAND // 2, 2, NFFT)[:, :, : NFFT // 2] / (32.0 * ROOT)
    table = np.swapaxes(table, 0, 1)
    table = np.concatenate([table.real, table.imag], axis=1)
    return table.astype(np.float32).astype(ml_dtypes.bfloat16)


def far_first(step, size):
    return size // 2 + (1 - 2 * (step % 2)) * ((step + 1) // 2)


class Partners:
    def __init__(self):
        station = lax.axis_index("station")
        block = lax.axis_index("tblock")
        self.z = lax.rem(station, 8)
        x = lax.div(block, 2) * 2 + lax.rem(lax.div(station, 8), 2)
        y = lax.div(station, 16)
        core = lax.rem(block, 2)
        xs, ys = {}, {}
        for d in range(4):
            there = lax.rem(x + d, 4)
            xs[d] = (lax.rem(there, 2) * 8, lax.div(there, 2) * 2)
            ys[d] = lax.rem(y + d, 4) * 16
        offsets = [(dx, dy, dc) for dx in range(4) for dy in range(4) for dc in (1, 0)]
        offsets.sort(key=lambda o: -(min(o[0], 4 - o[0]) + min(o[1], 4 - o[1])))
        self.plane = []
        for dx, dy, dc in offsets:
            low, high = xs[dx]
            self.plane.append((ys[dy] + low, high + (core if dc == 0 else 1 - core)))

    def layer(self, step):
        if isinstance(step, int):
            shift = far_first(step, 8)
        else:
            odd = lax.rem(step, 2)
            shift = 4 + (1 - 2 * odd) * lax.div(step + 1, 2)
        z = lax.rem(self.z + shift, 8)
        found = [(base + z, block) for base, block in self.plane]
        return found[:-1] if isinstance(step, int) and step == 7 else found


def exchange_kernel(
    v_hbm,
    proto_hbm,
    w_hbm,
    moved,
    proto_ref,
    v_buf,
    w_buf,
    sums,
    differences,
    first_quad,
    rows_buf,
    edge_out,
    edge_in,
    leaving,
    proto_sem,
    chunk_sem,
    w_sem,
    edge_send,
    edge_recv,
    send_sem,
    recv_sem,
):
    station = lax.axis_index("station")
    block = lax.axis_index("tblock")
    me = station * BLOCKS + block
    partners = Partners()
    barrier = pltpu.get_barrier_semaphore()

    def greet(step, part):
        for where in partners.layer(step)[part * 16 : part * 16 + 16]:
            pl.semaphore_signal(barrier, inc=1, device_id=where, device_id_type=MESH)

    def load(k, frames):
        for f in frames:
            for half in range(2):
                at = f * NFFT + half * HALF + k * CHUNK
                here = pl.ds(at if isinstance(f, int) else pl.multiple_of(at, CHUNK), CHUNK)
                pltpu.make_async_copy(
                    v_hbm.at[:, :, here], v_buf.at[:, :, here], chunk_sem.at[k]
                ).start()

    proto_copy = pltpu.make_async_copy(proto_hbm, proto_ref, proto_sem)
    proto_copy.start()
    greet(0, 0)
    load(0, range(FRAMES))
    greet(0, 1)
    load(1, range(FRAMES))
    w_copy = pltpu.make_async_copy(w_hbm, w_buf, w_sem)
    proto_copy.wait()

    def filter_tile(offset):
        spots = [pl.multiple_of(offset + half * HALF, LANES) for half in range(2)]
        taps = [
            [proto_ref[pl.ds(t, 1), pl.ds(spot, LANES)] for t in range(TAPS)] for spot in spots
        ]
        lanes = pl.ds(spots[0], LANES)
        for part in range(2):
            window = {}
            for s in range(FRAMES + EDGE):
                values = []
                for half in range(2):
                    value = None
                    for t in range(TAPS):
                        f = s + t - EDGE
                        if 0 <= f < FRAMES:
                            if (half, f) not in window:
                                at = pl.ds(pl.multiple_of(f * NFFT + spots[half], LANES), LANES)
                                window[half, f] = v_buf[part, :, at].astype(jnp.float32)
                            term = taps[half][t] * window[half, f]
                            value = term if value is None else value + term
                    values.append(value)
                row = (s // QUAD * 2 + part) * QUAD_ROWS + s % QUAD * INPUTS
                rows = pl.ds(row, INPUTS)
                sums[rows, lanes] = (values[0] + values[1]).astype(jnp.bfloat16)
                differences[rows, lanes] = (values[0] - values[1]).astype(jnp.bfloat16)

    for part in range(2):
        rows = pl.ds((2 * GROUPS - 2 + part) * QUAD_ROWS + EDGE * INPUTS, INPUTS)
        sums[rows, :] = jnp.zeros((INPUTS, HALF), jnp.bfloat16)
        differences[rows, :] = jnp.zeros((INPUTS, HALF), jnp.bfloat16)

    for k in range(CHUNKS):
        chunk = v_buf.at[:, :, pl.ds(0, 2 * FRAMES * CHUNK)]
        pltpu.make_async_copy(chunk, chunk, chunk_sem.at[k]).wait()
        turns = TILES // 2

        def two_tiles(turn, carry):
            for part in range(2):
                if not isinstance(turn, int) or k * turns + turn < 7:
                    greet(k * turns + turn + 1, part)
                if k + 2 < CHUNKS:
                    share = FRAMES // TILES
                    load(k + 2, [(turn * 2 + part) * share + f for f in range(share)])
                filter_tile(k * CHUNK + (turn * 2 + part) * LANES)
            return carry

        if k < CHUNKS - 1:
            lax.fori_loop(0, turns, two_tiles, 0)
        else:
            for turn in range(turns):
                two_tiles(turn, 0)
        if k == 1:
            w_copy.start()

    w_copy.wait()
    lane = lax.broadcasted_iota(jnp.int32, (PAIRS, LANES), 1)
    for parity, operand in enumerate((sums, differences)):
        total = lax.dot_general(
            w_buf[parity], operand[...], CONTRACT, preferred_element_type=jnp.float32
        )
        for group in range(GROUPS):
            own = total[:, group * LANES : (group + 1) * LANES]
            turned = pltpu.roll(own[PAIRS:], QUAD_ROWS, 1)
            value = own[:PAIRS] + jnp.where(lane < QUAD_ROWS, -turned, turned)
            if group == 0:
                first_quad[parity] = value
            elif group == GROUPS - 1:
                edge_out[parity] = value.astype(jnp.bfloat16)
            else:
                at = group // 2 * 2 * BAND + parity * 2 + group % 2
                rows_buf[pl.ds(at, PAIRS, stride=4), :] = value
    late = rows_buf[pl.ds(2 * BAND, 2 * BAND), :].reshape(BAND, 2, LANES)
    leaving[1] = late.astype(jnp.bfloat16)

    edge_copy = pltpu.make_async_remote_copy(
        src_ref=edge_out,
        dst_ref=edge_in,
        send_sem=edge_send,
        recv_sem=edge_recv,
        device_id=(station, lax.min(block + 1, BLOCKS - 1)),
        device_id_type=MESH,
    )

    @pl.when(block == 0)
    def _():
        edge_in[...] = jnp.zeros_like(edge_in)

    pl.semaphore_wait(barrier, DEVICES - 1)

    @pl.when(block < BLOCKS - 1)
    def _():
        edge_copy.start()

    def send(step, half):
        for where in partners.layer(step):
            pltpu.make_async_remote_copy(
                src_ref=leaving.at[half, where[0] * BLOCKS + where[1]],
                dst_ref=moved.at[half, me],
                send_sem=send_sem,
                recv_sem=recv_sem,
                device_id=where,
                device_id_type=MESH,
            ).start()

    def send_half(half):
        def layer(step, carry):
            send(step, half)
            return carry

        lax.fori_loop(0, 7, layer, 0)
        send(7, half)
        pltpu.make_async_copy(leaving.at[half, me], moved.at[half, me], recv_sem).start()

    send_half(1)

    @pl.when(block > 0)
    def _():
        edge_copy.wait_recv()

    for parity in range(2):
        value = first_quad[parity] + edge_in[parity].astype(jnp.float32)
        rows_buf[pl.ds(parity * 2, PAIRS, stride=4), :] = value
    early = rows_buf[pl.ds(0, 2 * BAND), :].reshape(BAND, 2, LANES)
    leaving[0] = early.astype(jnp.bfloat16)
    send_half(0)

    @pl.when(block < BLOCKS - 1)
    def _():
        edge_copy.wait_send()

    sent = leaving.at[:, pl.ds(0, DEVICES - 1)]
    pltpu.make_async_copy(sent, sent, send_sem).wait()
    pltpu.make_async_copy(moved, moved, recv_sem).wait()


def exchange(voltages, prototype, table):
    operands = (voltages, prototype, table)
    return pl.pallas_call(
        exchange_kernel,
        out_shape=jax.ShapeDtypeStruct((2, DEVICES, 2, LANES), jnp.bfloat16),
        in_specs=[pl.BlockSpec(memory_space=pltpu.HBM)] * 3,
        out_specs=pl.BlockSpec(memory_space=pl.ANY),
        scratch_shapes=[
            pltpu.VMEM((TAPS, NFFT), jnp.float32),
            pltpu.VMEM((2, INPUTS, FRAMES * NFFT), jnp.bfloat16),
            pltpu.VMEM((2, BAND, HALF), jnp.bfloat16),
            pltpu.VMEM((GROUPS * LANES, HALF), jnp.bfloat16),
            pltpu.VMEM((GROUPS * LANES, HALF), jnp.bfloat16),
            pltpu.VMEM((2, PAIRS, LANES), jnp.float32),
            pltpu.VMEM((4 * BAND, LANES), jnp.float32),
            pltpu.VMEM((2, PAIRS, LANES), jnp.bfloat16),
            pltpu.VMEM((2, PAIRS, LANES), jnp.bfloat16),
            pltpu.VMEM((2, DEVICES, 2, LANES), jnp.bfloat16),
            pltpu.SemaphoreType.DMA,
            pltpu.SemaphoreType.DMA((CHUNKS,)),
            pltpu.SemaphoreType.DMA,
            pltpu.SemaphoreType.DMA,
            pltpu.SemaphoreType.DMA,
            pltpu.SemaphoreType.DMA,
            pltpu.SemaphoreType.DMA,
        ],
        compiler_params=pltpu.CompilerParams(
            collective_id=0, has_side_effects=True, vmem_limit_bytes=32 * 1024 * 1024
        ),
        name="channelize_and_send",
    )(*[pltpu.with_memory_space_constraint(operand, pltpu.HBM) for operand in operands])


def correlate_kernel(moved_ref, out_hbm, moved, gathered, right, out_buf, out_sem):
    for half in range(2):
        rows = moved_ref[half].astype(jnp.float32).reshape(DEVICES * 2, LANES)
        moved[pl.ds(half * DEVICES * 2, DEVICES * 2), :] = rows
    lane = lax.broadcasted_iota(jnp.int32, (8, LANES), 1)
    row = lax.broadcasted_iota(jnp.int32, (8, LANES), 0)
    source = lax.rem(lane // INPUTS - row + 8, 8)
    back = lax.rem(lane + row * INPUTS, LANES)
    for group in range(8):
        columns = pl.ds(group * LANES, LANES)
        for block in range(BLOCKS):
            for quad in range(4):
                first = quad // 2 * DEVICES * 2 + group * 64 + block * 2 + quad % 2
                tile = moved[pl.ds(first, 8, stride=8), :]
                tile = pltpu.roll(tile, 0, 1, stride=INPUTS, stride_axis=0)
                tile = jnp.take_along_axis(tile, source, axis=0)
                tile = jnp.take_along_axis(tile, back, axis=1)
                at = (block * 4 + quad) * QUAD
                gathered[pl.ds(at, QUAD), columns] = tile[:QUAD]
                gathered[pl.ds(64 + at, QUAD), columns] = tile[QUAD:]
    right[...] = gathered[...].astype(jnp.bfloat16)

    wide = lax.broadcasted_iota(jnp.int32, (LANES, LANES), 1)
    copies = []
    for group in range(8):
        columns = pl.ds(group * LANES, LANES)
        square = gathered[:, columns].T
        other = pltpu.roll(square, 64, 1)
        other = jnp.where(wide < 64, other, -other)
        for part, left in enumerate((square, other)):
            product = jnp.dot(
                left.astype(jnp.bfloat16), right[...], preferred_element_type=jnp.float32
            )
            out_buf[0, part, columns, :] = (product * (1.0 / 64.0)).astype(jnp.bfloat16)
        copies.append(
            pltpu.make_async_copy(
                out_buf.at[:, :, columns, :], out_hbm.at[:, :, columns, :], out_sem.at[group]
            )
        )
        copies[-1].start()
    for copy in copies:
        copy.wait()


def correlate(moved):
    everyone = STATIONS * INPUTS
    shape = (1, 2, everyone, everyone)
    return pl.pallas_call(
        correlate_kernel,
        out_shape=jax.ShapeDtypeStruct(shape, jnp.bfloat16),
        in_specs=[pl.BlockSpec(memory_space=pltpu.VMEM)],
        out_specs=pl.BlockSpec(memory_space=pltpu.HBM),
        scratch_shapes=[
            pltpu.VMEM((DEVICES * 4, LANES), jnp.float32),
            pltpu.VMEM((LANES, everyone), jnp.float32),
            pltpu.VMEM((LANES, everyone), jnp.bfloat16),
            pltpu.VMEM(shape, jnp.bfloat16),
            pltpu.SemaphoreType.DMA((8,)),
        ],
        compiler_params=pltpu.CompilerParams(vmem_limit_bytes=32 * 1024 * 1024),
        name="correlate",
    )(moved)


def local(voltages, prototype):
    table = jnp.asarray(channel_table())
    return correlate(exchange(voltages, prototype, table))


def solution(mesh):
    return jax.shard_map(
        local,
        mesh=mesh,
        in_specs=(P(None, "station", "tblock"), P()),
        out_specs=P(("station", "tblock"), None, None, None),
        check_vma=False,
    )
```

```python
import math

import jax
import jax.numpy as jnp
import ml_dtypes
import numpy as np
from jax import lax
from jax.experimental import pallas as pl
from jax.experimental.pallas import tpu as pltpu
from jax.sharding import PartitionSpec as P

ROOT = 64
NFFT = 4096
TAPS = 4
BAND = 256
FRAMES = 16
INPUTS = 16
EDGE = TAPS - 1
QUAD = 4
QUAD_ROWS = QUAD * INPUTS
STATIONS = 64
BLOCKS = 4
DEVICES = STATIONS * BLOCKS
LANES = 128
HALF = NFFT // 2
PAIRS = BAND // 2
CHUNK = 512
CHUNKS = HALF // CHUNK
GROUPS = FRAMES // QUAD + 1
TILES = CHUNK // LANES
GREETED = 5
MESH = pl.DeviceIdType.MESH
CONTRACT = (((1,), (1,)), ((), ()))


def channel_table():
    def angles(first, second, period):
        product = (first[:, None] * second[None, :]) % period
        return product.astype(np.float32) * np.float32(2.0 * math.pi / period)

    def rounded(values):
        return values.astype(ml_dtypes.bfloat16).astype(np.float64)

    digits = np.arange(ROOT)
    first = angles(digits, digits, ROOT)
    root = rounded(np.cos(first)) - 1j * rounded(np.sin(first))
    twist_angle = angles(digits, digits, NFFT)
    twist = np.cos(twist_angle).astype(np.float64) - 1j * np.sin(twist_angle).astype(np.float64)
    high = (NFFT - BAND) // 2 // ROOT + np.arange(BAND // ROOT)
    table = (
        root.T[None, :, :, None] * twist.T[None, :, None, :] * root[:, high].T[:, None, None, :]
    )
    table = table.reshape(BAND // 2, 2, NFFT)[:, :, : NFFT // 2] / (32.0 * ROOT)
    table = np.swapaxes(table, 0, 1)
    table = np.concatenate([table.real, table.imag], axis=1)
    return table.astype(np.float32).astype(ml_dtypes.bfloat16)


def far_first(step, size):
    return size // 2 + (1 - 2 * (step % 2)) * ((step + 1) // 2)


class Partners:
    def __init__(self):
        station = lax.axis_index("station")
        block = lax.axis_index("tblock")
        self.z = lax.rem(station, 8)
        x = lax.div(block, 2) * 2 + lax.rem(lax.div(station, 8), 2)
        y = lax.div(station, 16)
        core = lax.rem(block, 2)
        xs, ys = {}, {}
        for d in range(4):
            there = lax.rem(x + d, 4)
            xs[d] = (lax.rem(there, 2) * 8, lax.div(there, 2) * 2)
            ys[d] = lax.rem(y + d, 4) * 16
        offsets = [(dx, dy, dc) for dx in range(4) for dy in range(4) for dc in (1, 0)]
        offsets.sort(key=lambda o: -(min(o[0], 4 - o[0]) + min(o[1], 4 - o[1])))
        self.plane = []
        for dx, dy, dc in offsets:
            low, high = xs[dx]
            self.plane.append((ys[dy] + low, high + (core if dc == 0 else 1 - core)))

    def layer(self, step):
        if isinstance(step, int):
            shift = far_first(step, 8)
        else:
            odd = lax.rem(step, 2)
            shift = 4 + (1 - 2 * odd) * lax.div(step + 1, 2)
        z = lax.rem(self.z + shift, 8)
        found = [(base + z, block) for base, block in self.plane]
        return found[:-1] if isinstance(step, int) and step == 7 else found


def exchange_kernel(
    v_hbm,
    proto_hbm,
    w_hbm,
    moved,
    proto_ref,
    v_buf,
    w_buf,
    sums,
    differences,
    first_quad,
    rows_buf,
    edge_out,
    edge_in,
    leaving,
    proto_sem,
    chunk_sem,
    w_sem,
    edge_send,
    edge_recv,
    send_sem,
    recv_sem,
):
    station = lax.axis_index("station")
    block = lax.axis_index("tblock")
    me = station * BLOCKS + block
    partners = Partners()
    barrier = pltpu.get_barrier_semaphore()

    def greet(step, part):
        for where in partners.layer(step)[part * 16 : part * 16 + 16]:
            pl.semaphore_signal(barrier, inc=1, device_id=where, device_id_type=MESH)

    def load(k, frames):
        for f in frames:
            for half in range(2):
                at = f * NFFT + half * HALF + k * CHUNK
                here = pl.ds(at if isinstance(f, int) else pl.multiple_of(at, CHUNK), CHUNK)
                pltpu.make_async_copy(
                    v_hbm.at[:, :, here], v_buf.at[:, :, here], chunk_sem.at[k]
                ).start()

    proto_copy = pltpu.make_async_copy(proto_hbm, proto_ref, proto_sem)
    proto_copy.start()
    for step in range(GREETED):
        greet(step, 0)
        greet(step, 1)
        if step < 2:
            load(step, range(FRAMES))
    w_copy = pltpu.make_async_copy(w_hbm, w_buf, w_sem)
    proto_copy.wait()

    def filter_tile(offset):
        spots = [pl.multiple_of(offset + half * HALF, LANES) for half in range(2)]
        taps = [
            [proto_ref[pl.ds(t, 1), pl.ds(spot, LANES)] for t in range(TAPS)] for spot in spots
        ]
        lanes = pl.ds(spots[0], LANES)
        for part in range(2):
            window = {}
            for s in range(FRAMES + EDGE):
                values = []
                for half in range(2):
                    value = None
                    for t in range(TAPS):
                        f = s + t - EDGE
                        if 0 <= f < FRAMES:
                            if (half, f) not in window:
                                at = pl.ds(pl.multiple_of(f * NFFT + spots[half], LANES), LANES)
                                window[half, f] = v_buf[part, :, at].astype(jnp.float32)
                            term = taps[half][t] * window[half, f]
                            value = term if value is None else value + term
                    values.append(value)
                row = (s // QUAD * 2 + part) * QUAD_ROWS + s % QUAD * INPUTS
                rows = pl.ds(row, INPUTS)
                sums[rows, lanes] = (values[0] + values[1]).astype(jnp.bfloat16)
                differences[rows, lanes] = (values[0] - values[1]).astype(jnp.bfloat16)

    for part in range(2):
        rows = pl.ds((2 * GROUPS - 2 + part) * QUAD_ROWS + EDGE * INPUTS, INPUTS)
        sums[rows, :] = jnp.zeros((INPUTS, HALF), jnp.bfloat16)
        differences[rows, :] = jnp.zeros((INPUTS, HALF), jnp.bfloat16)

    for k in range(CHUNKS):
        chunk = v_buf.at[:, :, pl.ds(0, 2 * FRAMES * CHUNK)]
        pltpu.make_async_copy(chunk, chunk, chunk_sem.at[k]).wait()
        turns = TILES // 2

        def two_tiles(turn, carry):
            step = GREETED + k * turns + turn
            for part in range(2):
                if k == 0 or (k == 1 and turn == 0):
                    greet(step, part)
                if k + 2 < CHUNKS:
                    share = FRAMES // TILES
                    load(k + 2, [(turn * 2 + part) * share + f for f in range(share)])
                filter_tile(k * CHUNK + (turn * 2 + part) * LANES)
            return carry

        if k == 1:
            for turn in range(turns):
                two_tiles(turn, 0)
        else:
            lax.fori_loop(0, turns, two_tiles, 0)
        if k == 1:
            w_copy.start()

    w_copy.wait()
    lane = lax.broadcasted_iota(jnp.int32, (PAIRS, LANES), 1)
    def transform(first, last):
        for parity, operand in enumerate((sums, differences)):
            total = lax.dot_general(
                w_buf[parity],
                operand[pl.ds(first * LANES, (last - first) * LANES), :],
                CONTRACT,
                preferred_element_type=jnp.float32,
            )
            for group in range(first, last):
                own = total[:, (group - first) * LANES : (group - first + 1) * LANES]
                turned = pltpu.roll(own[PAIRS:], QUAD_ROWS, 1)
                value = own[:PAIRS] + jnp.where(lane < QUAD_ROWS, -turned, turned)
                if group == 0:
                    first_quad[parity] = value
                elif group == GROUPS - 1:
                    edge_out[parity] = value.astype(jnp.bfloat16)
                else:
                    at = group // 2 * 2 * BAND + parity * 2 + group % 2
                    rows_buf[pl.ds(at, PAIRS, stride=4), :] = value

    transform(2, GROUPS)
    late = rows_buf[pl.ds(2 * BAND, 2 * BAND), :].reshape(BAND, 2, LANES)
    leaving[1] = late.astype(jnp.bfloat16)

    edge_copy = pltpu.make_async_remote_copy(
        src_ref=edge_out,
        dst_ref=edge_in,
        send_sem=edge_send,
        recv_sem=edge_recv,
        device_id=(station, lax.min(block + 1, BLOCKS - 1)),
        device_id_type=MESH,
    )

    @pl.when(block == 0)
    def _():
        edge_in[...] = jnp.zeros_like(edge_in)

    pl.semaphore_wait(barrier, DEVICES - 1)

    @pl.when(block < BLOCKS - 1)
    def _():
        edge_copy.start()

    def send(step, half):
        for where in partners.layer(step):
            pltpu.make_async_remote_copy(
                src_ref=leaving.at[half, where[0] * BLOCKS + where[1]],
                dst_ref=moved.at[half, me],
                send_sem=send_sem,
                recv_sem=recv_sem,
                device_id=where,
                device_id_type=MESH,
            ).start()

    def send_planes(half, first, last):
        def plane(step, carry):
            send(step, half)
            return carry

        if first < 7:
            lax.fori_loop(first, min(last, 7), plane, 0)
        if last == 8:
            send(7, half)

    far = 4
    send_planes(1, 0, far)
    transform(0, 2)

    @pl.when(block == 2)
    def _():
        send_planes(1, far, 8)

    @pl.when(block > 0)
    def _():
        edge_copy.wait_recv()

    for parity in range(2):
        value = first_quad[parity] + edge_in[parity].astype(jnp.float32)
        rows_buf[pl.ds(parity * 2, PAIRS, stride=4), :] = value
    early = rows_buf[pl.ds(0, 2 * BAND), :].reshape(BAND, 2, LANES)
    leaving[0] = early.astype(jnp.bfloat16)
    send_planes(0, 0, far)

    @pl.when(block != 2)
    def _():
        send_planes(1, far, 8)

    send_planes(0, far, 8)
    for half in range(2):
        pltpu.make_async_copy(leaving.at[half, me], moved.at[half, me], recv_sem).start()

    @pl.when(block < BLOCKS - 1)
    def _():
        edge_copy.wait_send()

    sent = leaving.at[:, pl.ds(0, DEVICES - 1)]
    pltpu.make_async_copy(sent, sent, send_sem).wait()
    pltpu.make_async_copy(moved, moved, recv_sem).wait()


def exchange(voltages, prototype, table):
    operands = (voltages, prototype, table)
    return pl.pallas_call(
        exchange_kernel,
        out_shape=jax.ShapeDtypeStruct((2, DEVICES, 2, LANES), jnp.bfloat16),
        in_specs=[pl.BlockSpec(memory_space=pltpu.HBM)] * 3,
        out_specs=pl.BlockSpec(memory_space=pl.ANY),
        scratch_shapes=[
            pltpu.VMEM((TAPS, NFFT), jnp.float32),
            pltpu.VMEM((2, INPUTS, FRAMES * NFFT), jnp.bfloat16),
            pltpu.VMEM((2, BAND, HALF), jnp.bfloat16),
            pltpu.VMEM((GROUPS * LANES, HALF), jnp.bfloat16),
            pltpu.VMEM((GROUPS * LANES, HALF), jnp.bfloat16),
            pltpu.VMEM((2, PAIRS, LANES), jnp.float32),
            pltpu.VMEM((4 * BAND, LANES), jnp.float32),
            pltpu.VMEM((2, PAIRS, LANES), jnp.bfloat16),
            pltpu.VMEM((2, PAIRS, LANES), jnp.bfloat16),
            pltpu.VMEM((2, DEVICES, 2, LANES), jnp.bfloat16),
            pltpu.SemaphoreType.DMA,
            pltpu.SemaphoreType.DMA((CHUNKS,)),
            pltpu.SemaphoreType.DMA,
            pltpu.SemaphoreType.DMA,
            pltpu.SemaphoreType.DMA,
            pltpu.SemaphoreType.DMA,
            pltpu.SemaphoreType.DMA,
        ],
        compiler_params=pltpu.CompilerParams(
            collective_id=0, has_side_effects=True, vmem_limit_bytes=32 * 1024 * 1024
        ),
        name="channelize_and_send",
    )(*[pltpu.with_memory_space_constraint(operand, pltpu.HBM) for operand in operands])


def correlate_kernel(moved_ref, out_hbm, moved, gathered, right, out_buf, out_sem):
    for half in range(2):
        rows = moved_ref[half].astype(jnp.float32).reshape(DEVICES * 2, LANES)
        moved[pl.ds(half * DEVICES * 2, DEVICES * 2), :] = rows
    lane = lax.broadcasted_iota(jnp.int32, (8, LANES), 1)
    row = lax.broadcasted_iota(jnp.int32, (8, LANES), 0)
    source = lax.rem(lane // INPUTS - row + 8, 8)
    back = lax.rem(lane + row * INPUTS, LANES)
    for group in range(8):
        columns = pl.ds(group * LANES, LANES)
        for block in range(BLOCKS):
            for quad in range(4):
                first = quad // 2 * DEVICES * 2 + group * 64 + block * 2 + quad % 2
                tile = moved[pl.ds(first, 8, stride=8), :]
                tile = pltpu.roll(tile, 0, 1, stride=INPUTS, stride_axis=0)
                tile = jnp.take_along_axis(tile, source, axis=0)
                tile = jnp.take_along_axis(tile, back, axis=1)
                at = (block * 4 + quad) * QUAD
                gathered[pl.ds(at, QUAD), columns] = tile[:QUAD]
                gathered[pl.ds(64 + at, QUAD), columns] = tile[QUAD:]
    right[...] = gathered[...].astype(jnp.bfloat16)

    wide = lax.broadcasted_iota(jnp.int32, (LANES, LANES), 1)
    copies = []
    for group in range(8):
        columns = pl.ds(group * LANES, LANES)
        square = gathered[:, columns].T
        other = pltpu.roll(square, 64, 1)
        other = jnp.where(wide < 64, other, -other)
        for part, left in enumerate((square, other)):
            product = jnp.dot(
                left.astype(jnp.bfloat16), right[...], preferred_element_type=jnp.float32
            )
            out_buf[0, part, columns, :] = (product * (1.0 / 64.0)).astype(jnp.bfloat16)
        copies.append(
            pltpu.make_async_copy(
                out_buf.at[:, :, columns, :], out_hbm.at[:, :, columns, :], out_sem.at[group]
            )
        )
        copies[-1].start()
    for copy in copies:
        copy.wait()


def correlate(moved):
    everyone = STATIONS * INPUTS
    shape = (1, 2, everyone, everyone)
    return pl.pallas_call(
        correlate_kernel,
        out_shape=jax.ShapeDtypeStruct(shape, jnp.bfloat16),
        in_specs=[pl.BlockSpec(memory_space=pltpu.VMEM)],
        out_specs=pl.BlockSpec(memory_space=pltpu.HBM),
        scratch_shapes=[
            pltpu.VMEM((DEVICES * 4, LANES), jnp.float32),
            pltpu.VMEM((LANES, everyone), jnp.float32),
            pltpu.VMEM((LANES, everyone), jnp.bfloat16),
            pltpu.VMEM(shape, jnp.bfloat16),
            pltpu.SemaphoreType.DMA((8,)),
        ],
        compiler_params=pltpu.CompilerParams(vmem_limit_bytes=32 * 1024 * 1024),
        name="correlate",
    )(moved)


def local(voltages, prototype):
    table = jnp.asarray(channel_table())
    return correlate(exchange(voltages, prototype, table))


def solution(mesh):
    return jax.shard_map(
        local,
        mesh=mesh,
        in_specs=(P(None, "station", "tblock"), P()),
        out_specs=P(("station", "tblock"), None, None, None),
        check_vma=False,
    )
```

```python
import math

import jax
import jax.numpy as jnp
import ml_dtypes
import numpy as np
from jax import lax
from jax.experimental import pallas as pl
from jax.experimental.pallas import tpu as pltpu
from jax.sharding import PartitionSpec as P

ROOT = 64
NFFT = 4096
TAPS = 4
BAND = 256
FRAMES = 16
INPUTS = 16
EDGE = TAPS - 1
QUAD = 4
QUAD_ROWS = QUAD * INPUTS
STATIONS = 64
BLOCKS = 4
DEVICES = STATIONS * BLOCKS
LANES = 128
HALF = NFFT // 2
PAIRS = BAND // 2
CHUNK = 512
CHUNKS = HALF // CHUNK
GROUPS = FRAMES // QUAD + 1
TILES = CHUNK // LANES
FAR = ((0, 0, 5), (1, 0, 3))
NEAR = ((0, 5, 7), (1, 3, 5), (0, 7, 8), (1, 5, 7), (1, 7, 8))
MESH = pl.DeviceIdType.MESH
CONTRACT = (((1,), (1,)), ((), ()))


def channel_table():
    def angles(first, second, period):
        product = (first[:, None] * second[None, :]) % period
        return product.astype(np.float32) * np.float32(2.0 * math.pi / period)

    def rounded(values):
        return values.astype(ml_dtypes.bfloat16).astype(np.float64)

    digits = np.arange(ROOT)
    first = angles(digits, digits, ROOT)
    root = rounded(np.cos(first)) - 1j * rounded(np.sin(first))
    twist_angle = angles(digits, digits, NFFT)
    twist = np.cos(twist_angle).astype(np.float64) - 1j * np.sin(twist_angle).astype(np.float64)
    high = (NFFT - BAND) // 2 // ROOT + np.arange(BAND // ROOT)
    table = (
        root.T[None, :, :, None] * twist.T[None, :, None, :] * root[:, high].T[:, None, None, :]
    )
    table = table.reshape(BAND // 2, 2, NFFT)[:, :, : NFFT // 2] / (32.0 * ROOT)
    table = np.swapaxes(table, 0, 1)
    table = np.concatenate([table.real, table.imag], axis=1)
    return table.astype(np.float32).astype(ml_dtypes.bfloat16)


def far_first(step, size):
    return size // 2 + (1 - 2 * (step % 2)) * ((step + 1) // 2)


class Partners:
    def __init__(self):
        station = lax.axis_index("station")
        block = lax.axis_index("tblock")
        self.z = lax.rem(station, 8)
        x = lax.div(block, 2) * 2 + lax.rem(lax.div(station, 8), 2)
        y = lax.div(station, 16)
        core = lax.rem(block, 2)
        xs, ys = {}, {}
        for d in range(4):
            there = lax.rem(x + d, 4)
            xs[d] = (lax.rem(there, 2) * 8, lax.div(there, 2) * 2)
            ys[d] = lax.rem(y + d, 4) * 16
        offsets = [(dx, dy, dc) for dx in range(4) for dy in range(4) for dc in (1, 0)]
        offsets.sort(key=lambda o: -(min(o[0], 4 - o[0]) + min(o[1], 4 - o[1])))
        self.plane = []
        for dx, dy, dc in offsets:
            low, high = xs[dx]
            self.plane.append((ys[dy] + low, high + (core if dc == 0 else 1 - core)))

    def half_plane(self, step, part):
        if isinstance(step, int):
            shift = far_first(step, 8)
        else:
            odd = lax.rem(step, 2)
            shift = 4 + (1 - 2 * odd) * lax.div(step + 1, 2)
        z = lax.rem(self.z + shift, 8)
        found = [(base + z, block) for base, block in self.plane[part * 16 : part * 16 + 16]]
        return found[:-1] if isinstance(step, int) and (step, part) == (7, 1) else found


def exchange_kernel(
    v_hbm,
    proto_hbm,
    w_hbm,
    moved,
    proto_ref,
    v_buf,
    w_buf,
    sums,
    differences,
    first_quad,
    rows_buf,
    edge_out,
    edge_in,
    leaving,
    proto_sem,
    chunk_sem,
    w_sem,
    edge_send,
    edge_recv,
    send_sem,
    recv_sem,
):
    station = lax.axis_index("station")
    block = lax.axis_index("tblock")
    me = station * BLOCKS + block
    partners = Partners()
    barrier = pltpu.get_barrier_semaphore()

    def greet(step, part):
        for where in partners.half_plane(step, part):
            pl.semaphore_signal(barrier, inc=1, device_id=where, device_id_type=MESH)

    def load(k, frames):
        for f in frames:
            for half in range(2):
                at = f * NFFT + half * HALF + k * CHUNK
                here = pl.ds(at if isinstance(f, int) else pl.multiple_of(at, CHUNK), CHUNK)
                pltpu.make_async_copy(
                    v_hbm.at[:, :, here], v_buf.at[:, :, here], chunk_sem.at[k]
                ).start()

    proto_copy = pltpu.make_async_copy(proto_hbm, proto_ref, proto_sem)
    proto_copy.start()
    for step in range(2):
        greet(step, 0)
    load(0, range(FRAMES))
    for step in range(2, 5):
        greet(step, 0)
    load(1, range(FRAMES))
    for step in range(3):
        greet(step, 1)
    w_copy = pltpu.make_async_copy(w_hbm, w_buf, w_sem)
    proto_copy.wait()

    def filter_tile(offset):
        spots = [pl.multiple_of(offset + half * HALF, LANES) for half in range(2)]
        taps = [
            [proto_ref[pl.ds(t, 1), pl.ds(spot, LANES)] for t in range(TAPS)] for spot in spots
        ]
        lanes = pl.ds(spots[0], LANES)
        for part in range(2):
            window = {}
            for s in range(FRAMES + EDGE):
                values = []
                for half in range(2):
                    value = None
                    for t in range(TAPS):
                        f = s + t - EDGE
                        if 0 <= f < FRAMES:
                            if (half, f) not in window:
                                at = pl.ds(pl.multiple_of(f * NFFT + spots[half], LANES), LANES)
                                window[half, f] = v_buf[part, :, at].astype(jnp.float32)
                            term = taps[half][t] * window[half, f]
                            value = term if value is None else value + term
                    values.append(value)
                row = (s // QUAD * 2 + part) * QUAD_ROWS + s % QUAD * INPUTS
                rows = pl.ds(row, INPUTS)
                sums[rows, lanes] = (values[0] + values[1]).astype(jnp.bfloat16)
                differences[rows, lanes] = (values[0] - values[1]).astype(jnp.bfloat16)

    for part in range(2):
        rows = pl.ds((2 * GROUPS - 2 + part) * QUAD_ROWS + EDGE * INPUTS, INPUTS)
        sums[rows, :] = jnp.zeros((INPUTS, HALF), jnp.bfloat16)
        differences[rows, :] = jnp.zeros((INPUTS, HALF), jnp.bfloat16)

    for k in range(CHUNKS):
        chunk = v_buf.at[:, :, pl.ds(0, 2 * FRAMES * CHUNK)]
        pltpu.make_async_copy(chunk, chunk, chunk_sem.at[k]).wait()
        turns = TILES // 2

        def two_tiles(turn, carry):
            for part in range(2):
                if k == 0:
                    greet(3 + turn if part else 5 + turn, part)
                elif k == 1:
                    greet(*((7, 0), (5, 1), (6, 1), (7, 1))[turn * 2 + part])
                if k + 2 < CHUNKS:
                    share = FRAMES // TILES
                    load(k + 2, [(turn * 2 + part) * share + f for f in range(share)])
                filter_tile(k * CHUNK + (turn * 2 + part) * LANES)
            return carry

        if k == 1:
            for turn in range(turns):
                two_tiles(turn, 0)
        else:
            lax.fori_loop(0, turns, two_tiles, 0)
        if k == 1:
            w_copy.start()

    w_copy.wait()
    lane = lax.broadcasted_iota(jnp.int32, (PAIRS, LANES), 1)
    def transform(first, last):
        for parity, operand in enumerate((sums, differences)):
            total = lax.dot_general(
                w_buf[parity],
                operand[pl.ds(first * LANES, (last - first) * LANES), :],
                CONTRACT,
                preferred_element_type=jnp.float32,
            )
            for group in range(first, last):
                own = total[:, (group - first) * LANES : (group - first + 1) * LANES]
                turned = pltpu.roll(own[PAIRS:], QUAD_ROWS, 1)
                value = own[:PAIRS] + jnp.where(lane < QUAD_ROWS, -turned, turned)
                if group == 0:
                    first_quad[parity] = value
                elif group == GROUPS - 1:
                    edge_out[parity] = value.astype(jnp.bfloat16)
                else:
                    at = group // 2 * 2 * BAND + parity * 2 + group % 2
                    rows_buf[pl.ds(at, PAIRS, stride=4), :] = value

    transform(2, GROUPS)
    late = rows_buf[pl.ds(2 * BAND, 2 * BAND), :].reshape(BAND, 2, LANES)
    leaving[1] = late.astype(jnp.bfloat16)

    edge_copy = pltpu.make_async_remote_copy(
        src_ref=edge_out,
        dst_ref=edge_in,
        send_sem=edge_send,
        recv_sem=edge_recv,
        device_id=(station, lax.min(block + 1, BLOCKS - 1)),
        device_id_type=MESH,
    )

    @pl.when(block == 0)
    def _():
        edge_in[...] = jnp.zeros_like(edge_in)

    pl.semaphore_wait(barrier, DEVICES - 1)

    @pl.when(block < BLOCKS - 1)
    def _():
        edge_copy.start()

    def send(runs, half):
        def half_plane(step, part):
            for where in partners.half_plane(step, part):
                pltpu.make_async_remote_copy(
                    src_ref=leaving.at[half, where[0] * BLOCKS + where[1]],
                    dst_ref=moved.at[half, me],
                    send_sem=send_sem,
                    recv_sem=recv_sem,
                    device_id=where,
                    device_id_type=MESH,
                ).start()

        for part, first, last in runs:
            if last == 8:
                half_plane(7, part)
            else:

                def body(step, carry):
                    half_plane(step, part)
                    return carry

                lax.fori_loop(first, last, body, 0)

    send(FAR, 1)
    transform(0, 2)

    @pl.when(block == 2)
    def _():
        send(NEAR, 1)

    @pl.when(block > 0)
    def _():
        edge_copy.wait_recv()

    for parity in range(2):
        value = first_quad[parity] + edge_in[parity].astype(jnp.float32)
        rows_buf[pl.ds(parity * 2, PAIRS, stride=4), :] = value
    early = rows_buf[pl.ds(0, 2 * BAND), :].reshape(BAND, 2, LANES)
    leaving[0] = early.astype(jnp.bfloat16)
    send(FAR, 0)

    @pl.when(block != 2)
    def _():
        send(NEAR, 1)

    send(NEAR, 0)
    for half in range(2):
        pltpu.make_async_copy(leaving.at[half, me], moved.at[half, me], recv_sem).start()

    @pl.when(block < BLOCKS - 1)
    def _():
        edge_copy.wait_send()

    sent = leaving.at[:, pl.ds(0, DEVICES - 1)]
    pltpu.make_async_copy(sent, sent, send_sem).wait()
    pltpu.make_async_copy(moved, moved, recv_sem).wait()


def exchange(voltages, prototype, table):
    operands = (voltages, prototype, table)
    return pl.pallas_call(
        exchange_kernel,
        out_shape=jax.ShapeDtypeStruct((2, DEVICES, 2, LANES), jnp.bfloat16),
        in_specs=[pl.BlockSpec(memory_space=pltpu.HBM)] * 3,
        out_specs=pl.BlockSpec(memory_space=pl.ANY),
        scratch_shapes=[
            pltpu.VMEM((TAPS, NFFT), jnp.float32),
            pltpu.VMEM((2, INPUTS, FRAMES * NFFT), jnp.bfloat16),
            pltpu.VMEM((2, BAND, HALF), jnp.bfloat16),
            pltpu.VMEM((GROUPS * LANES, HALF), jnp.bfloat16),
            pltpu.VMEM((GROUPS * LANES, HALF), jnp.bfloat16),
            pltpu.VMEM((2, PAIRS, LANES), jnp.float32),
            pltpu.VMEM((4 * BAND, LANES), jnp.float32),
            pltpu.VMEM((2, PAIRS, LANES), jnp.bfloat16),
            pltpu.VMEM((2, PAIRS, LANES), jnp.bfloat16),
            pltpu.VMEM((2, DEVICES, 2, LANES), jnp.bfloat16),
            pltpu.SemaphoreType.DMA,
            pltpu.SemaphoreType.DMA((CHUNKS,)),
            pltpu.SemaphoreType.DMA,
            pltpu.SemaphoreType.DMA,
            pltpu.SemaphoreType.DMA,
            pltpu.SemaphoreType.DMA,
            pltpu.SemaphoreType.DMA,
        ],
        compiler_params=pltpu.CompilerParams(
            collective_id=0, has_side_effects=True, vmem_limit_bytes=32 * 1024 * 1024
        ),
        name="channelize_and_send",
    )(*[pltpu.with_memory_space_constraint(operand, pltpu.HBM) for operand in operands])


def correlate_kernel(moved_ref, out_hbm, moved, gathered, right, out_buf, out_sem):
    for half in range(2):
        rows = moved_ref[half].astype(jnp.float32).reshape(DEVICES * 2, LANES)
        moved[pl.ds(half * DEVICES * 2, DEVICES * 2), :] = rows
    lane = lax.broadcasted_iota(jnp.int32, (8, LANES), 1)
    row = lax.broadcasted_iota(jnp.int32, (8, LANES), 0)
    source = lax.rem(lane // INPUTS - row + 8, 8)
    back = lax.rem(lane + row * INPUTS, LANES)
    for group in range(8):
        columns = pl.ds(group * LANES, LANES)
        for block in range(BLOCKS):
            for quad in range(4):
                first = quad // 2 * DEVICES * 2 + group * 64 + block * 2 + quad % 2
                tile = moved[pl.ds(first, 8, stride=8), :]
                tile = pltpu.roll(tile, 0, 1, stride=INPUTS, stride_axis=0)
                tile = jnp.take_along_axis(tile, source, axis=0)
                tile = jnp.take_along_axis(tile, back, axis=1)
                at = (block * 4 + quad) * QUAD
                gathered[pl.ds(at, QUAD), columns] = tile[:QUAD]
                gathered[pl.ds(64 + at, QUAD), columns] = tile[QUAD:]
    right[...] = gathered[...].astype(jnp.bfloat16)

    wide = lax.broadcasted_iota(jnp.int32, (LANES, LANES), 1)
    copies = []
    size = 1 * LANES
    for turn in range(8 // 1):
        lefts = ([], [])
        for group in range(turn * 1, turn * 1 + 1):
            square = gathered[:, pl.ds(group * LANES, LANES)].T
            other = pltpu.roll(square, 64, 1)
            lefts[0].append(square.astype(jnp.bfloat16))
            lefts[1].append(jnp.where(wide < 64, other, -other).astype(jnp.bfloat16))
        product = jnp.dot(
            jnp.concatenate(lefts[0] + lefts[1], axis=0),
            right[...],
            preferred_element_type=jnp.float32,
        )
        rows = pl.ds(turn * size, size)
        for part in range(2):
            out_buf[0, part, rows, :] = (
                product[part * size : (part + 1) * size] * (1.0 / 64.0)
            ).astype(jnp.bfloat16)
        copies.append(
            pltpu.make_async_copy(
                out_buf.at[:, :, rows, :], out_hbm.at[:, :, rows, :], out_sem.at[turn]
            )
        )
        copies[-1].start()
    for copy in copies:
        copy.wait()


def correlate(moved):
    everyone = STATIONS * INPUTS
    shape = (1, 2, everyone, everyone)
    return pl.pallas_call(
        correlate_kernel,
        out_shape=jax.ShapeDtypeStruct(shape, jnp.bfloat16),
        in_specs=[pl.BlockSpec(memory_space=pltpu.VMEM)],
        out_specs=pl.BlockSpec(memory_space=pltpu.HBM),
        scratch_shapes=[
            pltpu.VMEM((DEVICES * 4, LANES), jnp.float32),
            pltpu.VMEM((LANES, everyone), jnp.float32),
            pltpu.VMEM((LANES, everyone), jnp.bfloat16),
            pltpu.VMEM(shape, jnp.bfloat16),
            pltpu.SemaphoreType.DMA((8,)),
        ],
        compiler_params=pltpu.CompilerParams(vmem_limit_bytes=32 * 1024 * 1024),
        name="correlate",
    )(moved)


def local(voltages, prototype):
    table = jnp.asarray(channel_table())
    return correlate(exchange(voltages, prototype, table))


def solution(mesh):
    return jax.shard_map(
        local,
        mesh=mesh,
        in_specs=(P(None, "station", "tblock"), P()),
        out_specs=P(("station", "tblock"), None, None, None),
        check_vma=False,
    )
```

```python
import math

import jax
import jax.numpy as jnp
import ml_dtypes
import numpy as np
from jax import lax
from jax.experimental import pallas as pl
from jax.experimental.pallas import tpu as pltpu
from jax.sharding import PartitionSpec as P

ROOT = 64
NFFT = 4096
TAPS = 4
BAND = 256
FRAMES = 16
INPUTS = 16
EDGE = TAPS - 1
QUAD = 4
QUAD_ROWS = QUAD * INPUTS
STATIONS = 64
BLOCKS = 4
DEVICES = STATIONS * BLOCKS
LANES = 128
HALF = NFFT // 2
PAIRS = BAND // 2
CHUNK = 512
CHUNKS = HALF // CHUNK
GROUPS = FRAMES // QUAD + 1
TILES = CHUNK // LANES
FAR = ((0, 0, 5), (1, 0, 3))
NEAR = ((0, 5, 7), (1, 3, 5), (0, 7, 8), (1, 5, 7), (1, 7, 8))
MESH = pl.DeviceIdType.MESH
CONTRACT = (((1,), (1,)), ((), ()))


def channel_table():
    def angles(first, second, period):
        product = (first[:, None] * second[None, :]) % period
        return product.astype(np.float32) * np.float32(2.0 * math.pi / period)

    def rounded(values):
        return values.astype(ml_dtypes.bfloat16).astype(np.float64)

    digits = np.arange(ROOT)
    first = angles(digits, digits, ROOT)
    root = rounded(np.cos(first)) - 1j * rounded(np.sin(first))
    twist_angle = angles(digits, digits, NFFT)
    twist = np.cos(twist_angle).astype(np.float64) - 1j * np.sin(twist_angle).astype(np.float64)
    high = (NFFT - BAND) // 2 // ROOT + np.arange(BAND // ROOT)
    table = (
        root.T[None, :, :, None] * twist.T[None, :, None, :] * root[:, high].T[:, None, None, :]
    )
    table = table.reshape(BAND // 2, 2, NFFT)[:, :, : NFFT // 2] / (32.0 * ROOT)
    table = np.swapaxes(table, 0, 1)
    table = np.concatenate([table.real, table.imag], axis=1)
    return table.astype(np.float32).astype(ml_dtypes.bfloat16)


def far_first(step, size):
    return size // 2 + (1 - 2 * (step % 2)) * ((step + 1) // 2)


class Partners:
    def __init__(self):
        station = lax.axis_index("station")
        block = lax.axis_index("tblock")
        self.z = lax.rem(station, 8)
        x = lax.div(block, 2) * 2 + lax.rem(lax.div(station, 8), 2)
        y = lax.div(station, 16)
        core = lax.rem(block, 2)
        xs, ys = {}, {}
        for d in range(4):
            there = lax.rem(x + d, 4)
            xs[d] = (lax.rem(there, 2) * 8, lax.div(there, 2) * 2)
            ys[d] = lax.rem(y + d, 4) * 16
        offsets = [(dx, dy, dc) for dx in range(4) for dy in range(4) for dc in (1, 0)]
        offsets.sort(key=lambda o: -(min(o[0], 4 - o[0]) + min(o[1], 4 - o[1])))
        self.plane = []
        for dx, dy, dc in offsets:
            low, high = xs[dx]
            self.plane.append((ys[dy] + low, high + (core if dc == 0 else 1 - core)))

    def half_plane(self, step, part):
        if isinstance(step, int):
            shift = far_first(step, 8)
        else:
            odd = lax.rem(step, 2)
            shift = 4 + (1 - 2 * odd) * lax.div(step + 1, 2)
        z = lax.rem(self.z + shift, 8)
        found = [(base + z, block) for base, block in self.plane[part * 16 : part * 16 + 16]]
        return found[:-1] if isinstance(step, int) and (step, part) == (7, 1) else found


def exchange_kernel(
    v_hbm,
    proto_hbm,
    w_hbm,
    moved,
    proto_ref,
    v_buf,
    w_buf,
    sums,
    differences,
    first_quad,
    rows_buf,
    edge_out,
    edge_in,
    leaving,
    proto_sem,
    chunk_sem,
    w_sem,
    edge_send,
    edge_recv,
    send_sem,
    recv_sem,
):
    station = lax.axis_index("station")
    block = lax.axis_index("tblock")
    me = station * BLOCKS + block
    partners = Partners()
    barrier = pltpu.get_barrier_semaphore()

    def greet(step, part):
        for where in partners.half_plane(step, part):
            pl.semaphore_signal(barrier, inc=1, device_id=where, device_id_type=MESH)

    def load(k, frames):
        for f in frames:
            for half in range(2):
                at = f * NFFT + half * HALF + k * CHUNK
                here = pl.ds(at if isinstance(f, int) else pl.multiple_of(at, CHUNK), CHUNK)
                pltpu.make_async_copy(
                    v_hbm.at[:, :, here], v_buf.at[:, :, here], chunk_sem.at[k]
                ).start()

    proto_copy = pltpu.make_async_copy(proto_hbm, proto_ref, proto_sem)
    proto_copy.start()
    for step in range(2):
        greet(step, 0)
    load(0, range(FRAMES))
    for step in range(2, 5):
        greet(step, 0)
    load(1, range(FRAMES))
    for step in range(3):
        greet(step, 1)
    w_copy = pltpu.make_async_copy(w_hbm, w_buf, w_sem)
    proto_copy.wait()

    def filter_tile(offset):
        spots = [pl.multiple_of(offset + half * HALF, LANES) for half in range(2)]
        taps = [
            [proto_ref[pl.ds(t, 1), pl.ds(spot, LANES)] for t in range(TAPS)] for spot in spots
        ]
        lanes = pl.ds(spots[0], LANES)
        for part in range(2):
            window = {}
            for s in range(FRAMES + EDGE):
                values = []
                for half in range(2):
                    value = None
                    for t in range(TAPS):
                        f = s + t - EDGE
                        if 0 <= f < FRAMES:
                            if (half, f) not in window:
                                at = pl.ds(pl.multiple_of(f * NFFT + spots[half], LANES), LANES)
                                window[half, f] = v_buf[part, :, at].astype(jnp.float32)
                            term = taps[half][t] * window[half, f]
                            value = term if value is None else value + term
                    values.append(value)
                row = (s // QUAD * 2 + part) * QUAD_ROWS + s % QUAD * INPUTS
                rows = pl.ds(row, INPUTS)
                sums[rows, lanes] = (values[0] + values[1]).astype(jnp.bfloat16)
                differences[rows, lanes] = (values[0] - values[1]).astype(jnp.bfloat16)

    for part in range(2):
        rows = pl.ds((2 * GROUPS - 2 + part) * QUAD_ROWS + EDGE * INPUTS, INPUTS)
        sums[rows, :] = jnp.zeros((INPUTS, HALF), jnp.bfloat16)
        differences[rows, :] = jnp.zeros((INPUTS, HALF), jnp.bfloat16)

    for k in range(CHUNKS):
        chunk = v_buf.at[:, :, pl.ds(0, 2 * FRAMES * CHUNK)]
        pltpu.make_async_copy(chunk, chunk, chunk_sem.at[k]).wait()
        turns = TILES // 2

        def two_tiles(turn, carry):
            for part in range(2):
                if k == 0:
                    greet(3 + turn if part else 5 + turn, part)
                elif k == 1:
                    greet(*((7, 0), (5, 1), (6, 1), (7, 1))[turn * 2 + part])
                if k + 2 < CHUNKS:
                    share = FRAMES // TILES
                    load(k + 2, [(turn * 2 + part) * share + f for f in range(share)])
                filter_tile(k * CHUNK + (turn * 2 + part) * LANES)
            return carry

        if k == 1:
            for turn in range(turns):
                two_tiles(turn, 0)
        else:
            lax.fori_loop(0, turns, two_tiles, 0)
        if k == 0:
            w_copy.start()

    w_copy.wait()
    lane = lax.broadcasted_iota(jnp.int32, (PAIRS, LANES), 1)
    def transform(first, last):
        for parity, operand in enumerate((sums, differences)):
            total = lax.dot_general(
                w_buf[parity],
                operand[pl.ds(first * LANES, (last - first) * LANES), :],
                CONTRACT,
                preferred_element_type=jnp.float32,
            )
            for group in range(first, last):
                own = total[:, (group - first) * LANES : (group - first + 1) * LANES]
                turned = pltpu.roll(own[PAIRS:], QUAD_ROWS, 1)
                value = own[:PAIRS] + jnp.where(lane < QUAD_ROWS, -turned, turned)
                if group == 0:
                    first_quad[parity] = value
                elif group == GROUPS - 1:
                    edge_out[parity] = value.astype(jnp.bfloat16)
                else:
                    at = group // 2 * 2 * BAND + parity * 2 + group % 2
                    rows_buf[pl.ds(at, PAIRS, stride=4), :] = value

    transform(2, GROUPS)
    late = rows_buf[pl.ds(2 * BAND, 2 * BAND), :].reshape(BAND, 2, LANES)
    leaving[1] = late.astype(jnp.bfloat16)

    edge_copy = pltpu.make_async_remote_copy(
        src_ref=edge_out,
        dst_ref=edge_in,
        send_sem=edge_send,
        recv_sem=edge_recv,
        device_id=(station, lax.min(block + 1, BLOCKS - 1)),
        device_id_type=MESH,
    )

    @pl.when(block == 0)
    def _():
        edge_in[...] = jnp.zeros_like(edge_in)

    pl.semaphore_wait(barrier, DEVICES - 1)

    @pl.when(block < BLOCKS - 1)
    def _():
        edge_copy.start()

    def send(runs, half):
        def half_plane(step, part):
            for where in partners.half_plane(step, part):
                pltpu.make_async_remote_copy(
                    src_ref=leaving.at[half, where[0] * BLOCKS + where[1]],
                    dst_ref=moved.at[half, me],
                    send_sem=send_sem,
                    recv_sem=recv_sem,
                    device_id=where,
                    device_id_type=MESH,
                ).start()

        for part, first, last in runs:
            if last == 8:
                half_plane(7, part)
            else:

                def body(step, carry):
                    half_plane(step, part)
                    return carry

                lax.fori_loop(first, last, body, 0)

    send(FAR, 1)
    transform(0, 2)

    @pl.when(block == 2)
    def _():
        send(NEAR, 1)

    @pl.when(block > 0)
    def _():
        edge_copy.wait_recv()

    for parity in range(2):
        value = first_quad[parity] + edge_in[parity].astype(jnp.float32)
        rows_buf[pl.ds(parity * 2, PAIRS, stride=4), :] = value
    early = rows_buf[pl.ds(0, 2 * BAND), :].reshape(BAND, 2, LANES)
    leaving[0] = early.astype(jnp.bfloat16)
    send(FAR, 0)

    @pl.when(block != 2)
    def _():
        send(NEAR, 1)

    send(NEAR, 0)
    for half in range(2):
        pltpu.make_async_copy(leaving.at[half, me], moved.at[half, me], recv_sem).start()

    @pl.when(block < BLOCKS - 1)
    def _():
        edge_copy.wait_send()

    sent = leaving.at[:, pl.ds(0, DEVICES - 1)]
    pltpu.make_async_copy(sent, sent, send_sem).wait()
    pltpu.make_async_copy(moved, moved, recv_sem).wait()


def exchange(voltages, prototype, table):
    operands = (voltages, prototype, table)
    return pl.pallas_call(
        exchange_kernel,
        out_shape=jax.ShapeDtypeStruct((2, DEVICES, 2, LANES), jnp.bfloat16),
        in_specs=[pl.BlockSpec(memory_space=pltpu.HBM)] * 3,
        out_specs=pl.BlockSpec(memory_space=pl.ANY),
        scratch_shapes=[
            pltpu.VMEM((TAPS, NFFT), jnp.float32),
            pltpu.VMEM((2, INPUTS, FRAMES * NFFT), jnp.bfloat16),
            pltpu.VMEM((2, BAND, HALF), jnp.bfloat16),
            pltpu.VMEM((GROUPS * LANES, HALF), jnp.bfloat16),
            pltpu.VMEM((GROUPS * LANES, HALF), jnp.bfloat16),
            pltpu.VMEM((2, PAIRS, LANES), jnp.float32),
            pltpu.VMEM((4 * BAND, LANES), jnp.float32),
            pltpu.VMEM((2, PAIRS, LANES), jnp.bfloat16),
            pltpu.VMEM((2, PAIRS, LANES), jnp.bfloat16),
            pltpu.VMEM((2, DEVICES, 2, LANES), jnp.bfloat16),
            pltpu.SemaphoreType.DMA,
            pltpu.SemaphoreType.DMA((CHUNKS,)),
            pltpu.SemaphoreType.DMA,
            pltpu.SemaphoreType.DMA,
            pltpu.SemaphoreType.DMA,
            pltpu.SemaphoreType.DMA,
            pltpu.SemaphoreType.DMA,
        ],
        compiler_params=pltpu.CompilerParams(
            collective_id=0, has_side_effects=True, vmem_limit_bytes=32 * 1024 * 1024
        ),
        name="channelize_and_send",
    )(*[pltpu.with_memory_space_constraint(operand, pltpu.HBM) for operand in operands])


def correlate_kernel(moved_ref, out_hbm, moved, gathered, right, out_buf, out_sem):
    for half in range(2):
        rows = moved_ref[half].astype(jnp.float32).reshape(DEVICES * 2, LANES)
        moved[pl.ds(half * DEVICES * 2, DEVICES * 2), :] = rows
    lane = lax.broadcasted_iota(jnp.int32, (8, LANES), 1)
    row = lax.broadcasted_iota(jnp.int32, (8, LANES), 0)
    source = lax.rem(lane // INPUTS - row + 8, 8)
    back = lax.rem(lane + row * INPUTS, LANES)
    for group in range(8):
        columns = pl.ds(group * LANES, LANES)
        for block in range(BLOCKS):
            for quad in range(4):
                first = quad // 2 * DEVICES * 2 + group * 64 + block * 2 + quad % 2
                tile = moved[pl.ds(first, 8, stride=8), :]
                tile = pltpu.roll(tile, 0, 1, stride=INPUTS, stride_axis=0)
                tile = jnp.take_along_axis(tile, source, axis=0)
                tile = jnp.take_along_axis(tile, back, axis=1)
                gathered[pl.ds((block * 4 + quad) * 8, 8), columns] = tile
    right[...] = gathered[...].astype(jnp.bfloat16)

    imaginary = lax.rem(lax.broadcasted_iota(jnp.int32, (LANES, LANES), 1), 8) >= QUAD
    copies = []
    size = 1 * LANES
    for turn in range(8 // 1):
        lefts = ([], [])
        for group in range(turn * 1, turn * 1 + 1):
            square = gathered[:, pl.ds(group * LANES, LANES)].T
            forward, backward = pltpu.roll(square, LANES - QUAD, 1), pltpu.roll(square, QUAD, 1)
            lefts[0].append(square.astype(jnp.bfloat16))
            lefts[1].append(jnp.where(imaginary, -backward, forward).astype(jnp.bfloat16))
        product = jnp.dot(
            jnp.concatenate(lefts[0] + lefts[1], axis=0),
            right[...],
            preferred_element_type=jnp.float32,
        )
        rows = pl.ds(turn * size, size)
        for part in range(2):
            out_buf[0, part, rows, :] = (
                product[part * size : (part + 1) * size] * (1.0 / 64.0)
            ).astype(jnp.bfloat16)
        copies.append(
            pltpu.make_async_copy(
                out_buf.at[:, :, rows, :], out_hbm.at[:, :, rows, :], out_sem.at[turn]
            )
        )
        copies[-1].start()
    for copy in copies:
        copy.wait()


def correlate(moved):
    everyone = STATIONS * INPUTS
    shape = (1, 2, everyone, everyone)
    return pl.pallas_call(
        correlate_kernel,
        out_shape=jax.ShapeDtypeStruct(shape, jnp.bfloat16),
        in_specs=[pl.BlockSpec(memory_space=pltpu.VMEM)],
        out_specs=pl.BlockSpec(memory_space=pltpu.HBM),
        scratch_shapes=[
            pltpu.VMEM((DEVICES * 4, LANES), jnp.float32),
            pltpu.VMEM((LANES, everyone), jnp.float32),
            pltpu.VMEM((LANES, everyone), jnp.bfloat16),
            pltpu.VMEM(shape, jnp.bfloat16),
            pltpu.SemaphoreType.DMA((8,)),
        ],
        compiler_params=pltpu.CompilerParams(vmem_limit_bytes=32 * 1024 * 1024),
        name="correlate",
    )(moved)


def local(voltages, prototype):
    table = jnp.asarray(channel_table())
    return correlate(exchange(voltages, prototype, table))


def solution(mesh):
    return jax.shard_map(
        local,
        mesh=mesh,
        in_specs=(P(None, "station", "tblock"), P()),
        out_specs=P(("station", "tblock"), None, None, None),
        check_vma=False,
    )
```
